32 devices in a mesh: row: 4 (over x, core), col: 8 (over z, y).
Axes of the slice: x: 2, y: 2, z: 4, core: 2. Of those that a mesh axis runs over, the one named last changes fastest.
Arguments:
- features: bfloat16 [64, 128, 1024], P(None, 'row', 'col'), may hold values from -6 to 6
- patch_index: int32 [128, 1024], P('row', 'col'), may hold values from 0 to 2047
- confidence: float32 [128, 1024], P('row', 'col'), may hold values from 0.2 to 1
- bank: bfloat16 [32, 576, 2048], P(('row', 'col')), may hold values from -6 to 6
- page_owner: int32 [2], replicated, may hold values from 0 to 31
- texture_weight: bfloat16 [64, 576], replicated, may hold values from -0.25 to 0.25
- conv_weight: bfloat16 [8, 9, 64, 64], replicated, may hold values from -0.25 to 0.25
Outputs:
- restored: bfloat16 [64, 128, 1024], P(None, 'row', 'col')
The draws below stay inside these ranges and needn't reach their ends.
Inputs may be any that keep to these rules, and one draw needn't show every extreme that they name: `patch_index`: each entry is a patch number of the page. `page_owner`: each entry is a slot number.
All inputs are finite; a program needn't handle non-finite values.
Results may differ from the reference program's by a relative error of at most 0.024.
Values may be sent and summed in bfloat16 or wider, within the bound.
A program may use at most 128 MiB of HBM per device.

```python
import jax
import jax.numpy as jnp
from jax import lax

C = 64
BANKW = 576
PATCHES = 2048
LAYERS = 8
STEPS = 2
SLOTS = 32
HEIGHT = 128
WIDTH = 1024


def set_ends(array, own_key, least, high):
    dims = array.shape
    place = [jax.random.randint(jax.random.fold_in(own_key, axis), (), 0, dims[axis]) for axis in range(len(dims))]
    array = array.at[tuple(place)].set(least)
    longest = dims.index(max(dims))
    place[longest] = (place[longest] + 1) % dims[longest]
    return array.at[tuple(place)].set(high)


def level_of(own_key, shape, pieces, smallest, top_value):
    def one(axis_at, blocks):
        draws = jax.random.uniform(jax.random.fold_in(jax.random.fold_in(own_key, 6), axis_at), (blocks,), jnp.float32, smallest / len(pieces), top_value / len(pieces))
        return jnp.repeat(jnp.exp(draws), shape[axis_at] // blocks).reshape((-1,) + (1,) * (len(shape) - axis_at - 1))

    gain = one(*pieces[0])
    for cut in pieces[1:]:
        gain = gain * one(*cut)
    return gain


def bell_draw(own_key, shape, deviation, reach, split=(), kind=jnp.bfloat16):
    level = level_of(own_key, shape, split, -0.22, 0.18) if split else 1.0
    entries = jax.random.normal(own_key, shape, jnp.float32) * deviation * level
    return jnp.minimum(jnp.maximum(entries, -reach), reach).astype(kind)


def setup_inputs(seed: int = 0) -> dict:
    streams_of = jax.random.split(jax.random.key(seed), 8)
    features = bell_draw(streams_of[0], (C, HEIGHT, WIDTH), 1.0, 6.0, ((1, 4), (2, 8)))
    patch_index = set_ends(jax.random.randint(streams_of[1], (HEIGHT, WIDTH), 0, PATCHES), jax.random.fold_in(streams_of[1], 1), 0, PATCHES - 1).astype(jnp.int32)
    confidence = jnp.clip(0.2 + 0.8 * jax.random.uniform(streams_of[2], (HEIGHT, WIDTH), jnp.float32) ** level_of(streams_of[2], (HEIGHT, WIDTH), ((0, 4), (1, 8)), -0.2, 0.2), 0.2, 1.0)
    bank = bell_draw(streams_of[3], (SLOTS, BANKW, PATCHES), 1.0, 6.0, ((0, 32),))
    page_owner = jax.random.randint(streams_of[4], (STEPS,), 0, SLOTS).astype(jnp.int32)
    texture_weight = bell_draw(streams_of[5], (C, BANKW), BANKW ** -0.5, 0.25)
    conv_weight = bell_draw(streams_of[6], (LAYERS, 9, C, C), (9 * C) ** -0.5, 0.25)
    return {"features": features, "patch_index": patch_index, "confidence": confidence, "bank": bank, "page_owner": page_owner, "texture_weight": texture_weight, "conv_weight": conv_weight}


def convolve(field, kernel):
    taps = kernel.astype(jnp.float32).reshape(3, 3, C, C).transpose(2, 3, 0, 1)
    out = lax.conv_general_dilated(field.astype(jnp.float32)[None], taps, (1, 1), ((1, 1), (1, 1)), dimension_numbers=("NCHW", "OIHW", "NCHW"))
    return out[0]


def reference(features, patch_index, confidence, bank, page_owner, texture_weight, conv_weight):
    state = features
    for step in range(STEPS):
        page = lax.dynamic_index_in_dim(bank, page_owner[step], 0, keepdims=False)
        projected = jnp.dot(texture_weight, page, preferred_element_type=jnp.float32).astype(jnp.bfloat16)
        texture = jnp.take(projected, patch_index.reshape(-1), axis=1).reshape(C, HEIGHT, WIDTH)
        state = (state.astype(jnp.float32) + confidence[None] * texture.astype(jnp.float32)).astype(jnp.bfloat16)
        for block in range(LAYERS // 2):
            inner = jnp.maximum(convolve(state, conv_weight[2 * block]), 0.0).astype(jnp.bfloat16)
            state = (state.astype(jnp.float32) + convolve(inner, conv_weight[2 * block + 1])).astype(jnp.bfloat16)
    return state
```

```python
import functools

import jax
import jax.numpy as jnp
from jax import lax
from jax.experimental import pallas as pl
from jax.experimental.pallas import tpu as pltpu
from jax.sharding import PartitionSpec as P

LAYERS = 8
STEPS = 2
HALO = LAYERS * STEPS
LOW = 256
SLICE = 16
AROUND = [(-1, -1), (-1, 0), (-1, 1), (0, -1), (0, 1), (1, -1), (1, 0), (1, 1)]
MESH = pl.DeviceIdType.MESH
VMEM = pl.BlockSpec(memory_space=pltpu.VMEM)
SMEM = pl.BlockSpec(memory_space=pltpu.SMEM)


def project_kernel(weight_ref, bank_ref, out_ref):
    out_ref[...] = jnp.dot(
        weight_ref[...], bank_ref[0], preferred_element_type=jnp.float32
    ).astype(jnp.bfloat16)


def project(texture_weight, bank):
    chans, depth = texture_weight.shape
    high = bank.shape[2] // LOW
    return pl.pallas_call(
        project_kernel,
        grid=(high,),
        in_specs=[
            pl.BlockSpec((chans, depth), lambda h: (0, 0)),
            pl.BlockSpec((1, depth, LOW), lambda h: (0, 0, h)),
        ],
        out_specs=pl.BlockSpec((chans, LOW), lambda h: (h, 0)),
        out_shape=jax.ShapeDtypeStruct((high * chans, LOW), jnp.bfloat16),
    )(texture_weight, bank)


def exchange_kernel(
    rows, cols, hubs,
    owner_ref, proj_ref, state_ref, left_ref, right_ref, aux_ref,
    pages_ref, above_ref, below_ref, onleft_ref, onright_ref, around_ref,
    slots, spread_send, spread_recv, gather_send, gather_recv,
    halo_send, halo_recv, aux_send, aux_recv,
):
    my_row, my_col = lax.axis_index("row"), lax.axis_index("col")
    count = rows * cols
    me = my_row * cols + my_col

    def place(index):
        return (index // cols, lax.rem(index, cols))

    def spread(source_slice, slot, target):
        return pltpu.make_async_remote_copy(
            src_ref=proj_ref.at[pl.ds(pl.multiple_of(source_slice * SLICE, SLICE), SLICE), :],
            dst_ref=slots.at[slot],
            send_sem=spread_send.at[target],
            recv_sem=spread_recv.at[slot],
            device_id=place(target),
            device_id_type=MESH,
        )

    def gather(part, target):
        part_ref = pages_ref.at[:, pl.ds(pl.multiple_of(part * SLICE, SLICE), SLICE), :]
        return pltpu.make_async_remote_copy(
            src_ref=part_ref,
            dst_ref=part_ref,
            send_sem=gather_send.at[target],
            recv_sem=gather_recv.at[part],
            device_id=place(target),
            device_id_type=MESH,
        )

    def each_other(limit, action):
        def step(k, carry):
            other = lax.rem(me + k, count)
            if limit == count:
                action(other)
            else:
                pl.when(other < limit)(lambda: action(other))
            return carry

        lax.fori_loop(1, count, step, 0)

    def if_hub(action):
        if hubs == count:
            action()
        else:
            pl.when(me < hubs)(action)

    half = HALO
    quarter = left_ref.shape[0] // 2

    def halo(k):
        dr, dc = AROUND[k]
        if dc == 0:
            source = state_ref.at[pl.ds(0 if dr < 0 else half, half)]
            dest = below_ref if dr < 0 else above_ref
        else:
            edge = left_ref if dc < 0 else right_ref
            land = onright_ref if dc < 0 else onleft_ref
            if dr == 0:
                source, dest = edge, land.at[pl.ds(quarter, 2 * quarter)]
            elif dr < 0:
                source, dest = edge.at[pl.ds(0, quarter)], land.at[pl.ds(3 * quarter, quarter)]
            else:
                source, dest = edge.at[pl.ds(quarter, quarter)], land.at[pl.ds(0, quarter)]
        target = (lax.rem(my_row + dr + rows, rows), lax.rem(my_col + dc + cols, cols))
        first = pltpu.make_async_remote_copy(
            src_ref=source, dst_ref=dest, send_sem=halo_send.at[k], recv_sem=halo_recv.at[k],
            device_id=target, device_id_type=MESH,
        )
        second = pltpu.make_async_remote_copy(
            src_ref=aux_ref, dst_ref=around_ref.at[7 - k], send_sem=aux_send.at[k],
            recv_sem=aux_recv.at[k], device_id=target, device_id_type=MESH,
        )
        return first, second

    each_other(hubs, lambda other: spread(other, me, other).start())
    halos = [copy for k in range(8) for copy in halo(k)]
    for copy in halos:
        copy.start()

    def pick():
        slots[me] = proj_ref[pl.ds(pl.multiple_of(me * SLICE, SLICE), SLICE), :]
        each_other(count, lambda other: spread(0, other, other).wait_recv())
        for step in range(STEPS):
            pages_ref[step, pl.ds(pl.multiple_of(me * SLICE, SLICE), SLICE), :] = slots[
                owner_ref[step]
            ]
        each_other(count, lambda other: gather(me, other).start())

    if_hub(pick)
    each_other(hubs, lambda other: spread(other, me, other).wait_send())
    each_other(hubs, lambda other: gather(other, other).wait_recv())
    if_hub(lambda: each_other(count, lambda other: gather(me, other).wait_send()))
    for copy in halos:
        copy.wait()


def exchange(rows, cols, page_owner, proj, state, left, right, aux):
    count = rows * cols
    hubs = min(count, proj.shape[0] // SLICE)
    tile_h, chans, tile_w = state.shape
    edge = (2 * left.shape[0],) + left.shape[1:]
    bf16 = jnp.bfloat16
    dma = pltpu.SemaphoreType.DMA
    return pl.pallas_call(
        functools.partial(exchange_kernel, rows, cols, hubs),
        in_specs=[SMEM] + [VMEM] * 5,
        out_specs=[VMEM] * 6,
        out_shape=[
            jax.ShapeDtypeStruct((STEPS,) + proj.shape, bf16),
            jax.ShapeDtypeStruct((HALO, chans, tile_w), bf16),
            jax.ShapeDtypeStruct((HALO, chans, tile_w), bf16),
            jax.ShapeDtypeStruct(edge, bf16),
            jax.ShapeDtypeStruct(edge, bf16),
            jax.ShapeDtypeStruct((8,) + aux.shape, jnp.float32),
        ],
        scratch_shapes=[
            pltpu.VMEM((count, SLICE, LOW), bf16),
            dma((count,)), dma((count,)), dma((count,)), dma((count,)),
            dma((8,)), dma((8,)), dma((8,)), dma((8,)),
        ],
        compiler_params=pltpu.CompilerParams(
            has_side_effects=True, vmem_limit_bytes=32 * 1024 * 1024
        ),
    )(page_owner, proj, state, left, right, aux)


def trunk_kernel(
    rows, cols,
    pages_ref, state_ref, above_ref, below_ref, onleft_ref, onright_ref, aux_ref, around_ref,
    weight_ref, out_ref,
    field, inner, second, patch, trust,
):
    my_row, my_col = lax.axis_index("row"), lax.axis_index("col")
    tile_h, chans, tile_w = state_ref.shape
    full_h, lanes = tile_h + 2 * HALO, 2 * tile_w
    per = tile_w // HALO
    half = tile_w // 2

    lane = lax.broadcasted_iota(jnp.int32, (1, lanes), 1)
    column = jnp.where(lane < lanes - half, lane, lane - lanes)
    in_view = (column >= -HALO) & (column < tile_w + HALO)
    column = column + my_col * tile_w
    in_cols = in_view & (column >= 0) & (column < cols * tile_w)
    top = my_row * tile_h - HALO

    def keep(i):
        row = top + i
        inside = (row >= 0) & (row < rows * tile_h)
        return jnp.where(in_cols, inside.astype(jnp.int32), 0) > 0

    narrow = lax.broadcasted_iota(jnp.int32, (1, tile_w), 1) < half
    for which, target in ((0, patch), (1, trust)):
        for start, size, begin, trio in (
            (0, HALO, tile_h - HALO, (0, 1, 2)),
            (HALO, tile_h, 0, (3, None, 4)),
            (HALO + tile_h, HALO, 0, (5, 6, 7)),
        ):
            low, mid, high = [
                (aux_ref if k is None else around_ref.at[k])[which, pl.ds(begin, size), :]
                for k in trio
            ]
            target[pl.ds(start, size), :tile_w] = mid
            target[pl.ds(start, size), tile_w:] = jnp.where(narrow, high, low)

    row_of = lax.broadcasted_iota(jnp.int32, (LOW, lanes), 0)
    count_high = pages_ref.shape[1] // chans

    def begin_row(ref, at, group, spot, i):
        number = patch[pl.ds(i, 1), :].astype(jnp.int32)
        high = lax.shift_right_logical(number, 8)
        hot = jnp.where(row_of == (number & (LOW - 1)), 1.0, 0.0).astype(jnp.bfloat16)
        values = []
        for step in range(STEPS):
            every = jnp.dot(pages_ref[step], hot, preferred_element_type=jnp.float32)
            value = every[:chans]
            for h in range(1, count_high):
                value = jnp.where(high == h, every[h * chans : (h + 1) * chans], value)
            values.append(value)
        main = ref[at].astype(jnp.float32)
        right = pltpu.roll(onright_ref[group].astype(jnp.float32), (tile_w - spot * HALO) % tile_w, 1)
        left = pltpu.roll(onleft_ref[group].astype(jnp.float32), tile_w - HALO - spot * HALO, 1)
        start = jnp.concatenate([main, jnp.where(narrow, right, left)], axis=1)
        start = start + trust[pl.ds(i, 1), :] * values[0]
        field[i + 1] = jnp.where(keep(i), start, 0.0).astype(jnp.bfloat16)
        second[i] = values[1].astype(jnp.bfloat16)

    for ref, start, size in ((above_ref, 0, HALO), (state_ref, HALO, tile_h), (below_ref, HALO + tile_h, HALO)):
        def begin_group(g, carry, ref=ref, start=start):
            for spot in range(per):
                begin_row(ref, g * per + spot, start // per + g, spot, start + g * per + spot)
            return carry

        lax.fori_loop(0, size // per, begin_group, 0)

    unroll = 4
    for layer in range(STEPS * LAYERS):
        source, target = (field, inner) if layer % 2 == 0 else (inner, field)
        if layer == LAYERS:
            def again(i, carry):
                value = field[i + 1].astype(jnp.float32)
                value = value + trust[pl.ds(i, 1), :] * second[i].astype(jnp.float32)
                field[i + 1] = jnp.where(keep(i), value, 0.0).astype(jnp.bfloat16)
                return carry

            lax.fori_loop(layer, full_h - layer, again, 0)
        first = layer - layer % 2
        total = full_h - 2 * first

        def conv_rows(g, carry, layer=layer, first=first, source=source, target=target):
            early, late = carry
            kernel = weight_ref[layer % LAYERS]
            for u in range(unroll):
                r = first + g * unroll + u
                value = source[r + 1]
                stacked = jnp.concatenate(
                    [pltpu.roll(value, 1, 1), value, pltpu.roll(value, lanes - 1, 1)], axis=0
                )
                product = jnp.dot(kernel, stacked, preferred_element_type=jnp.float32)
                done = late + product[2 * chans :]
                late = early + product[chans : 2 * chans]
                early = product[:chans]
                if layer % 2 == 0:
                    done = jnp.maximum(done, 0.0)
                else:
                    done = field[r].astype(jnp.float32) + done
                target[r] = jnp.where(keep(r - 1), done, 0.0).astype(jnp.bfloat16)
            return early, late

        zero = jnp.zeros((chans, lanes), jnp.float32)
        lax.fori_loop(0, total // unroll, conv_rows, (zero, zero))

    out_ref[...] = field[pl.ds(HALO + 1, tile_h), :, :tile_w]


def trunk(rows, cols, pages, state, above, below, onleft, onright, aux, around, weights):
    tile_h, chans, tile_w = state.shape
    full_h, lanes = tile_h + 2 * HALO, 2 * tile_w
    return pl.pallas_call(
        functools.partial(trunk_kernel, rows, cols),
        in_specs=[VMEM] * 9,
        out_specs=VMEM,
        out_shape=jax.ShapeDtypeStruct(state.shape, jnp.bfloat16),
        scratch_shapes=[
            pltpu.VMEM((full_h + 2, chans, lanes), jnp.bfloat16),
            pltpu.VMEM((full_h + 2, chans, lanes), jnp.bfloat16),
            pltpu.VMEM((full_h, chans, lanes), jnp.bfloat16),
            pltpu.VMEM((full_h, lanes), jnp.float32),
            pltpu.VMEM((full_h, lanes), jnp.float32),
        ],
        compiler_params=pltpu.CompilerParams(vmem_limit_bytes=48 * 1024 * 1024),
    )(pages, state, above, below, onleft, onright, aux, around, weights)


def packed(edge, tile_w):
    tile_h, chans, width = edge.shape
    per = tile_w // width
    return edge.reshape(tile_h // per, per, chans, width).transpose(0, 2, 1, 3).reshape(
        tile_h // per, chans, tile_w
    )


def body(rows, cols, features, patch_index, confidence, bank, page_owner, texture_weight, conv_weight):
    chans, tile_h, tile_w = features.shape
    proj = project(texture_weight, bank)
    state = features.transpose(1, 0, 2)
    left = packed(state[:, :, :HALO], tile_w)
    right = packed(state[:, :, tile_w - HALO :], tile_w)
    aux = jnp.stack([patch_index.astype(jnp.float32), confidence])
    weights = (
        conv_weight.reshape(LAYERS, 3, 3, chans, chans)
        .transpose(0, 1, 3, 2, 4)
        .reshape(LAYERS, 3 * chans, 3 * chans)
    )
    received = exchange(rows, cols, page_owner, proj, state, left, right, aux)
    pages, above, below, onleft, onright, around = received
    out = trunk(rows, cols, pages, state, above, below, onleft, onright, aux, around, weights)
    return out.transpose(1, 0, 2)


def solution(mesh):
    return jax.shard_map(
        functools.partial(body, mesh.shape["row"], mesh.shape["col"]),
        mesh=mesh,
        in_specs=(
            P(None, "row", "col"),
            P("row", "col"),
            P("row", "col"),
            P(("row", "col"), None, None),
            P(),
            P(),
            P(),
        ),
        out_specs=P(None, "row", "col"),
        check_vma=False,
    )
```

```python
import functools

import jax
import jax.numpy as jnp
from jax import lax
from jax.experimental import pallas as pl
from jax.experimental.pallas import tpu as pltpu
from jax.sharding import PartitionSpec as P

LAYERS = 8
STEPS = 2
HALO = LAYERS * STEPS
UNROLL = 32
LOW = 256
SLICE = 16
AROUND = [(-1, -1), (-1, 0), (-1, 1), (0, -1), (0, 1), (1, -1), (1, 0), (1, 1)]
MESH = pl.DeviceIdType.MESH
VMEM = pl.BlockSpec(memory_space=pltpu.VMEM)
SMEM = pl.BlockSpec(memory_space=pltpu.SMEM)


def project_kernel(weight_ref, bank_ref, out_ref):
    out_ref[...] = jnp.dot(
        weight_ref[...], bank_ref[0], preferred_element_type=jnp.float32
    ).astype(jnp.bfloat16)


def project(texture_weight, bank):
    chans, depth = texture_weight.shape
    high = bank.shape[2] // LOW
    return pl.pallas_call(
        project_kernel,
        grid=(high,),
        in_specs=[
            pl.BlockSpec((chans, depth), lambda h: (0, 0)),
            pl.BlockSpec((1, depth, LOW), lambda h: (0, 0, h)),
        ],
        out_specs=pl.BlockSpec((chans, LOW), lambda h: (h, 0)),
        out_shape=jax.ShapeDtypeStruct((high * chans, LOW), jnp.bfloat16),
    )(texture_weight, bank)


def exchange_kernel(
    rows, cols, hubs,
    owner_ref, proj_ref, state_ref, left_ref, right_ref, aux_ref, taps_ref,
    pages_ref, above_ref, below_ref, onleft_ref, onright_ref, around_ref, weight_ref,
    slots, spread_send, spread_recv, gather_send, gather_recv,
    halo_send, halo_recv, aux_send, aux_recv,
):
    my_row, my_col = lax.axis_index("row"), lax.axis_index("col")
    count = rows * cols
    me = my_row * cols + my_col

    def place(index):
        return (index // cols, lax.rem(index, cols))

    def spread(source_slice, slot, target):
        return pltpu.make_async_remote_copy(
            src_ref=proj_ref.at[pl.ds(pl.multiple_of(source_slice * SLICE, SLICE), SLICE), :],
            dst_ref=slots.at[slot],
            send_sem=spread_send.at[target],
            recv_sem=spread_recv.at[slot],
            device_id=place(target),
            device_id_type=MESH,
        )

    def gather(part, target):
        part_ref = pages_ref.at[:, pl.ds(pl.multiple_of(part * SLICE, SLICE), SLICE), :]
        return pltpu.make_async_remote_copy(
            src_ref=part_ref,
            dst_ref=part_ref,
            send_sem=gather_send.at[target],
            recv_sem=gather_recv.at[part],
            device_id=place(target),
            device_id_type=MESH,
        )

    def each_other(limit, action):
        def step(k, carry):
            other = lax.rem(me + k, count)
            if limit == count:
                action(other)
            else:
                pl.when(other < limit)(lambda: action(other))
            return carry

        lax.fori_loop(1, count, step, 0)

    def if_hub(action):
        if hubs == count:
            action()
        else:
            pl.when(me < hubs)(action)

    half = HALO
    quarter = left_ref.shape[0] // 2

    def halo(k):
        dr, dc = AROUND[k]
        if dc == 0:
            source = state_ref.at[pl.ds(0 if dr < 0 else half, half)]
            dest = below_ref if dr < 0 else above_ref
        else:
            edge = left_ref if dc < 0 else right_ref
            land = onright_ref if dc < 0 else onleft_ref
            if dr == 0:
                source, dest = edge, land.at[pl.ds(quarter, 2 * quarter)]
            elif dr < 0:
                source, dest = edge.at[pl.ds(0, quarter)], land.at[pl.ds(3 * quarter, quarter)]
            else:
                source, dest = edge.at[pl.ds(quarter, quarter)], land.at[pl.ds(0, quarter)]
        target = (lax.rem(my_row + dr + rows, rows), lax.rem(my_col + dc + cols, cols))
        first = pltpu.make_async_remote_copy(
            src_ref=source, dst_ref=dest, send_sem=halo_send.at[k], recv_sem=halo_recv.at[k],
            device_id=target, device_id_type=MESH,
        )
        second = pltpu.make_async_remote_copy(
            src_ref=aux_ref, dst_ref=around_ref.at[7 - k], send_sem=aux_send.at[k],
            recv_sem=aux_recv.at[k], device_id=target, device_id_type=MESH,
        )
        return first, second

    each_other(hubs, lambda other: spread(other, me, other).start())
    def in_window(row, col):
        return (row >= 0) & (row < rows) & (col >= 0) & (col < cols)

    for k, (dr, dc) in enumerate(AROUND):
        @pl.when(in_window(my_row + dr, my_col + dc))
        def _(k=k):
            for copy in halo(k):
                copy.start()

    chans = taps_ref.shape[2]

    def arrange(layer, carry):
        for dy in range(3):
            weight_ref[layer, dy * chans : (dy + 1) * chans, :] = jnp.concatenate(
                [taps_ref[layer, 3 * dy + dx] for dx in range(3)], axis=1
            )
        return carry

    lax.fori_loop(0, LAYERS, arrange, 0)

    def pick():
        slots[me] = proj_ref[pl.ds(pl.multiple_of(me * SLICE, SLICE), SLICE), :]
        each_other(count, lambda other: spread(0, other, other).wait_recv())
        for step in range(STEPS):
            pages_ref[step, pl.ds(pl.multiple_of(me * SLICE, SLICE), SLICE), :] = slots[
                owner_ref[step]
            ]
        each_other(count, lambda other: gather(me, other).start())

    if_hub(pick)
    each_other(hubs, lambda other: spread(other, me, other).wait_send())
    each_other(hubs, lambda other: gather(other, other).wait_recv())
    if_hub(lambda: each_other(count, lambda other: gather(me, other).wait_send()))
    for k, (dr, dc) in enumerate(AROUND):
        @pl.when(in_window(my_row + dr, my_col + dc))
        def _(k=k):
            for copy in halo(k):
                copy.wait_send()

        @pl.when(in_window(my_row - dr, my_col - dc))
        def _(k=k):
            for copy in halo(k):
                copy.wait_recv()


def exchange(rows, cols, page_owner, proj, state, left, right, aux, taps):
    count = rows * cols
    hubs = min(count, proj.shape[0] // SLICE)
    tile_h, chans, tile_w = state.shape
    edge = (2 * left.shape[0],) + left.shape[1:]
    bf16 = jnp.bfloat16
    dma = pltpu.SemaphoreType.DMA
    return pl.pallas_call(
        functools.partial(exchange_kernel, rows, cols, hubs),
        in_specs=[SMEM] + [VMEM] * 6,
        out_specs=[VMEM] * 7,
        out_shape=[
            jax.ShapeDtypeStruct((STEPS,) + proj.shape, bf16),
            jax.ShapeDtypeStruct((HALO, chans, tile_w), bf16),
            jax.ShapeDtypeStruct((HALO, chans, tile_w), bf16),
            jax.ShapeDtypeStruct(edge, bf16),
            jax.ShapeDtypeStruct(edge, bf16),
            jax.ShapeDtypeStruct((8,) + aux.shape, jnp.float32),
            jax.ShapeDtypeStruct((LAYERS, 3 * chans, 3 * chans), bf16),
        ],
        scratch_shapes=[
            pltpu.VMEM((count, SLICE, LOW), bf16),
            dma((count,)), dma((count,)), dma((count,)), dma((count,)),
            dma((8,)), dma((8,)), dma((8,)), dma((8,)),
        ],
        compiler_params=pltpu.CompilerParams(
            has_side_effects=True, vmem_limit_bytes=32 * 1024 * 1024
        ),
    )(page_owner, proj, state, left, right, aux, taps)


def trunk_kernel(
    rows, cols,
    pages_ref, state_ref, above_ref, below_ref, onleft_ref, onright_ref, aux_ref, around_ref,
    weight_ref, out_ref,
    field, inner, second, patch, trust,
):
    my_row, my_col = lax.axis_index("row"), lax.axis_index("col")
    tile_h, chans, tile_w = state_ref.shape
    full_h, lanes = tile_h + 2 * HALO, 2 * tile_w
    per = tile_w // HALO
    half = tile_w // 2

    lane = lax.broadcasted_iota(jnp.int32, (1, lanes), 1)
    column = jnp.where(lane < lanes - half, lane, lane - lanes)
    in_view = (column >= -HALO) & (column < tile_w + HALO)
    column = column + my_col * tile_w
    in_cols = in_view & (column >= 0) & (column < cols * tile_w)
    top = my_row * tile_h - HALO

    def keep(i):
        row = top + i
        inside = (row >= 0) & (row < rows * tile_h)
        return jnp.where(in_cols, inside.astype(jnp.int32), 0) > 0

    narrow = lax.broadcasted_iota(jnp.int32, (1, tile_w), 1) < half
    for which, target in ((0, patch), (1, trust)):
        for start, size, begin, trio in (
            (0, HALO, tile_h - HALO, (0, 1, 2)),
            (HALO, tile_h, 0, (3, None, 4)),
            (HALO + tile_h, HALO, 0, (5, 6, 7)),
        ):
            low, mid, high = [
                (aux_ref if k is None else around_ref.at[k])[which, pl.ds(begin, size), :]
                for k in trio
            ]
            target[pl.ds(start, size), :tile_w] = mid
            target[pl.ds(start, size), tile_w:] = jnp.where(narrow, high, low)

    row_of = lax.broadcasted_iota(jnp.int32, (LOW, lanes), 0)
    count_high = pages_ref.shape[1] // chans

    def begin_row(ref, at, group, spot, i):
        number = patch[pl.ds(i, 1), :].astype(jnp.int32)
        high = lax.shift_right_logical(number, 8)
        hot = jnp.where(row_of == (number & (LOW - 1)), 1.0, 0.0).astype(jnp.bfloat16)
        values = []
        for step in range(STEPS):
            every = jnp.dot(pages_ref[step], hot, preferred_element_type=jnp.float32)
            value = every[:chans]
            for h in range(1, count_high):
                value = jnp.where(high == h, every[h * chans : (h + 1) * chans], value)
            values.append(value)
        main = ref[at].astype(jnp.float32)
        right = pltpu.roll(onright_ref[group].astype(jnp.float32), (tile_w - spot * HALO) % tile_w, 1)
        left = pltpu.roll(onleft_ref[group].astype(jnp.float32), tile_w - HALO - spot * HALO, 1)
        start = jnp.concatenate([main, jnp.where(narrow, right, left)], axis=1)
        start = start + trust[pl.ds(i, 1), :] * values[0]
        field[i + 1] = jnp.where(keep(i), start, 0.0).astype(jnp.bfloat16)
        second[i] = values[1].astype(jnp.bfloat16)

    for ref, start, size in ((above_ref, 0, HALO), (state_ref, HALO, tile_h), (below_ref, HALO + tile_h, HALO)):
        def begin_group(g, carry, ref=ref, start=start):
            for spot in range(per):
                begin_row(ref, g * per + spot, start // per + g, spot, start + g * per + spot)
            return carry

        lax.fori_loop(0, size // per, begin_group, 0)

    for layer in range(STEPS * LAYERS):
        source, target = (field, inner) if layer % 2 == 0 else (inner, field)
        if layer == LAYERS:
            def again(i, carry):
                value = field[i + 1].astype(jnp.float32)
                value = value + trust[pl.ds(i, 1), :] * second[i].astype(jnp.float32)
                field[i + 1] = jnp.where(keep(i), value, 0.0).astype(jnp.bfloat16)
                return carry

            lax.fori_loop(layer, full_h - layer, again, 0)
        first = layer - layer % 2
        total = full_h - 2 * first
        unroll = max(d for d in range(1, UNROLL + 1) if total % d == 0)

        def conv_rows(g, carry, layer=layer, unroll=unroll, first=first, source=source, target=target):
            early, late = carry
            kernel = weight_ref[layer % LAYERS]
            for u in range(unroll):
                r = first + g * unroll + u
                value = source[r + 1]
                stacked = jnp.concatenate(
                    [pltpu.roll(value, 1, 1), value, pltpu.roll(value, lanes - 1, 1)], axis=0
                )
                product = jnp.dot(kernel, stacked, preferred_element_type=jnp.float32)
                done = late + product[2 * chans :]
                late = early + product[chans : 2 * chans]
                early = product[:chans]
                if layer % 2 == 0:
                    done = jnp.maximum(done, 0.0)
                else:
                    done = field[r].astype(jnp.float32) + done
                target[r] = jnp.where(keep(r - 1), done, 0.0).astype(jnp.bfloat16)
            return early, late

        zero = jnp.zeros((chans, lanes), jnp.float32)
        lax.fori_loop(0, total // unroll, conv_rows, (zero, zero))

    out_ref[...] = field[pl.ds(HALO + 1, tile_h), :, :tile_w]


def trunk(rows, cols, pages, state, above, below, onleft, onright, aux, around, weights):
    tile_h, chans, tile_w = state.shape
    full_h, lanes = tile_h + 2 * HALO, 2 * tile_w
    return pl.pallas_call(
        functools.partial(trunk_kernel, rows, cols),
        in_specs=[VMEM] * 9,
        out_specs=VMEM,
        out_shape=jax.ShapeDtypeStruct(state.shape, jnp.bfloat16),
        scratch_shapes=[
            pltpu.VMEM((full_h + 2, chans, lanes), jnp.bfloat16),
            pltpu.VMEM((full_h + 2, chans, lanes), jnp.bfloat16),
            pltpu.VMEM((full_h, chans, lanes), jnp.bfloat16),
            pltpu.VMEM((full_h, lanes), jnp.float32),
            pltpu.VMEM((full_h, lanes), jnp.float32),
        ],
        compiler_params=pltpu.CompilerParams(vmem_limit_bytes=48 * 1024 * 1024),
    )(pages, state, above, below, onleft, onright, aux, around, weights)


def packed(edge, tile_w):
    tile_h, chans, width = edge.shape
    per = tile_w // width
    return edge.reshape(tile_h // per, per, chans, width).transpose(0, 2, 1, 3).reshape(
        tile_h // per, chans, tile_w
    )


def body(rows, cols, features, patch_index, confidence, bank, page_owner, texture_weight, conv_weight):
    chans, tile_h, tile_w = features.shape
    proj = project(texture_weight, bank)
    state = features.transpose(1, 0, 2)
    left = packed(state[:, :, :HALO], tile_w)
    right = packed(state[:, :, tile_w - HALO :], tile_w)
    aux = jnp.stack([patch_index.astype(jnp.float32), confidence])
    received = exchange(rows, cols, page_owner, proj, state, left, right, aux, conv_weight)
    pages, above, below, onleft, onright, around, weights = received
    out = trunk(rows, cols, pages, state, above, below, onleft, onright, aux, around, weights)
    return out.transpose(1, 0, 2)


def solution(mesh):
    return jax.shard_map(
        functools.partial(body, mesh.shape["row"], mesh.shape["col"]),
        mesh=mesh,
        in_specs=(
            P(None, "row", "col"),
            P("row", "col"),
            P("row", "col"),
            P(("row", "col"), None, None),
            P(),
            P(),
            P(),
        ),
        out_specs=P(None, "row", "col"),
        check_vma=False,
    )
```

```python
import functools

import jax
import jax.numpy as jnp
from jax import lax
from jax.experimental import pallas as pl
from jax.experimental.pallas import tpu as pltpu
from jax.sharding import PartitionSpec as P

LAYERS = 8
STEPS = 2
HALO = LAYERS * STEPS
UNROLL = 32
LOW = 256
SLICE = 16
AROUND = [(-1, -1), (-1, 0), (-1, 1), (0, -1), (0, 1), (1, -1), (1, 0), (1, 1)]
MESH = pl.DeviceIdType.MESH
VMEM = pl.BlockSpec(memory_space=pltpu.VMEM)
SMEM = pl.BlockSpec(memory_space=pltpu.SMEM)


def project_kernel(weight_ref, bank_ref, out_ref):
    chans = weight_ref.shape[0]
    for h in range(bank_ref.shape[2] // LOW):
        out_ref[h * chans : (h + 1) * chans, :] = jnp.dot(
            weight_ref[...],
            bank_ref[0, :, h * LOW : (h + 1) * LOW],
            preferred_element_type=jnp.float32,
        ).astype(jnp.bfloat16)


def project(texture_weight, bank):
    chans, depth = texture_weight.shape
    high = bank.shape[2] // LOW
    return pl.pallas_call(
        project_kernel,
        grid=(2,),
        in_specs=[
            pl.BlockSpec((chans, depth), lambda h: (0, 0)),
            pl.BlockSpec((1, depth, high // 2 * LOW), lambda h: (0, 0, h)),
        ],
        out_specs=pl.BlockSpec((high // 2 * chans, LOW), lambda h: (h, 0)),
        out_shape=jax.ShapeDtypeStruct((high * chans, LOW), jnp.bfloat16),
    )(texture_weight, bank)


def exchange_kernel(
    rows, cols, hubs,
    owner_ref, proj_ref, state_ref, left_ref, right_ref, aux_ref, taps_ref,
    pages_ref, above_ref, below_ref, onleft_ref, onright_ref, around_ref, weight_ref,
    slots, spread_send, spread_recv, gather_send, gather_recv,
    halo_send, halo_recv, aux_send, aux_recv,
):
    my_row, my_col = lax.axis_index("row"), lax.axis_index("col")
    count = rows * cols
    me = my_row * cols + my_col

    def place(index):
        return (index // cols, lax.rem(index, cols))

    def spread(source_slice, slot, target):
        return pltpu.make_async_remote_copy(
            src_ref=proj_ref.at[pl.ds(pl.multiple_of(source_slice * SLICE, SLICE), SLICE), :],
            dst_ref=slots.at[slot],
            send_sem=spread_send.at[target],
            recv_sem=spread_recv.at[slot],
            device_id=place(target),
            device_id_type=MESH,
        )

    def gather(part, target):
        part_ref = pages_ref.at[:, pl.ds(pl.multiple_of(part * SLICE, SLICE), SLICE), :]
        return pltpu.make_async_remote_copy(
            src_ref=part_ref,
            dst_ref=part_ref,
            send_sem=gather_send.at[target],
            recv_sem=gather_recv.at[part],
            device_id=place(target),
            device_id_type=MESH,
        )

    def each_other(limit, action):
        def step(k, carry):
            other = lax.rem(me + k, count)
            if limit == count:
                action(other)
            else:
                pl.when(other < limit)(lambda: action(other))
            return carry

        lax.fori_loop(1, count, step, 0)

    def if_hub(action):
        if hubs == count:
            action()
        else:
            pl.when(me < hubs)(action)

    half = HALO
    quarter = left_ref.shape[0] // 2

    def halo(k):
        dr, dc = AROUND[k]
        if dc == 0:
            source = state_ref.at[pl.ds(0 if dr < 0 else half, half)]
            dest = below_ref if dr < 0 else above_ref
        else:
            edge = left_ref if dc < 0 else right_ref
            land = onright_ref if dc < 0 else onleft_ref
            if dr == 0:
                source, dest = edge, land.at[pl.ds(quarter, 2 * quarter)]
            elif dr < 0:
                source, dest = edge.at[pl.ds(0, quarter)], land.at[pl.ds(3 * quarter, quarter)]
            else:
                source, dest = edge.at[pl.ds(quarter, quarter)], land.at[pl.ds(0, quarter)]
        target = (lax.rem(my_row + dr + rows, rows), lax.rem(my_col + dc + cols, cols))
        first = pltpu.make_async_remote_copy(
            src_ref=source, dst_ref=dest, send_sem=halo_send.at[k], recv_sem=halo_recv.at[k],
            device_id=target, device_id_type=MESH,
        )
        second = pltpu.make_async_remote_copy(
            src_ref=aux_ref, dst_ref=around_ref.at[7 - k], send_sem=aux_send.at[k],
            recv_sem=aux_recv.at[k], device_id=target, device_id_type=MESH,
        )
        return first, second

    each_other(hubs, lambda other: spread(other, me, other).start())
    def in_window(row, col):
        return (row >= 0) & (row < rows) & (col >= 0) & (col < cols)

    for k, (dr, dc) in enumerate(AROUND):
        @pl.when(in_window(my_row + dr, my_col + dc))
        def _(k=k):
            for copy in halo(k):
                copy.start()

    chans = taps_ref.shape[2]

    def arrange(layer, carry):
        for dy in range(3):
            weight_ref[layer, dy * chans : (dy + 1) * chans, :] = jnp.concatenate(
                [taps_ref[layer, 3 * dy + dx] for dx in range(3)], axis=1
            )
        return carry

    lax.fori_loop(0, LAYERS, arrange, 0)

    def pick():
        slots[me] = proj_ref[pl.ds(pl.multiple_of(me * SLICE, SLICE), SLICE), :]
        each_other(count, lambda other: spread(0, other, other).wait_recv())
        for step in range(STEPS):
            pages_ref[step, pl.ds(pl.multiple_of(me * SLICE, SLICE), SLICE), :] = slots[
                owner_ref[step]
            ]
        each_other(count, lambda other: gather(me, other).start())

    if_hub(pick)
    each_other(hubs, lambda other: spread(other, me, other).wait_send())
    each_other(hubs, lambda other: gather(other, other).wait_recv())
    if_hub(lambda: each_other(count, lambda other: gather(me, other).wait_send()))
    for k, (dr, dc) in enumerate(AROUND):
        @pl.when(in_window(my_row + dr, my_col + dc))
        def _(k=k):
            for copy in halo(k):
                copy.wait_send()

        @pl.when(in_window(my_row - dr, my_col - dc))
        def _(k=k):
            for copy in halo(k):
                copy.wait_recv()


def exchange(rows, cols, page_owner, proj, state, left, right, aux, taps):
    count = rows * cols
    hubs = min(count, proj.shape[0] // SLICE)
    tile_h, chans, tile_w = state.shape
    edge = (2 * left.shape[0],) + left.shape[1:]
    bf16 = jnp.bfloat16
    dma = pltpu.SemaphoreType.DMA
    return pl.pallas_call(
        functools.partial(exchange_kernel, rows, cols, hubs),
        in_specs=[SMEM] + [VMEM] * 6,
        out_specs=[VMEM] * 7,
        out_shape=[
            jax.ShapeDtypeStruct((STEPS,) + proj.shape, bf16),
            jax.ShapeDtypeStruct((HALO, chans, tile_w), bf16),
            jax.ShapeDtypeStruct((HALO, chans, tile_w), bf16),
            jax.ShapeDtypeStruct(edge, bf16),
            jax.ShapeDtypeStruct(edge, bf16),
            jax.ShapeDtypeStruct((8,) + aux.shape, jnp.float32),
            jax.ShapeDtypeStruct((LAYERS, 3 * chans, 3 * chans), bf16),
        ],
        scratch_shapes=[
            pltpu.VMEM((count, SLICE, LOW), bf16),
            dma((count,)), dma((count,)), dma((count,)), dma((count,)),
            dma((8,)), dma((8,)), dma((8,)), dma((8,)),
        ],
        compiler_params=pltpu.CompilerParams(
            has_side_effects=True, vmem_limit_bytes=32 * 1024 * 1024
        ),
    )(page_owner, proj, state, left, right, aux, taps)


def trunk_kernel(
    rows, cols,
    pages_ref, state_ref, above_ref, below_ref, onleft_ref, onright_ref, aux_ref, around_ref,
    weight_ref, out_ref,
    field, inner, second, patch, trust,
):
    my_row, my_col = lax.axis_index("row"), lax.axis_index("col")
    tile_h, chans, tile_w = state_ref.shape
    full_h, lanes = tile_h + 2 * HALO, 2 * tile_w
    per = tile_w // HALO
    half = tile_w // 2

    lane = lax.broadcasted_iota(jnp.int32, (1, lanes), 1)
    column = jnp.where(lane < lanes - half, lane, lane - lanes)
    in_view = (column >= -HALO) & (column < tile_w + HALO)
    column = column + my_col * tile_w
    in_cols = in_view & (column >= 0) & (column < cols * tile_w)
    top = my_row * tile_h - HALO

    def keep(i):
        row = top + i
        inside = (row >= 0) & (row < rows * tile_h)
        return jnp.where(in_cols, inside.astype(jnp.int32), 0) > 0

    narrow = lax.broadcasted_iota(jnp.int32, (1, tile_w), 1) < half
    for which, target in ((0, patch), (1, trust)):
        for start, size, begin, trio in (
            (0, HALO, tile_h - HALO, (0, 1, 2)),
            (HALO, tile_h, 0, (3, None, 4)),
            (HALO + tile_h, HALO, 0, (5, 6, 7)),
        ):
            low, mid, high = [
                (aux_ref if k is None else around_ref.at[k])[which, pl.ds(begin, size), :]
                for k in trio
            ]
            target[pl.ds(start, size), :tile_w] = mid
            target[pl.ds(start, size), tile_w:] = jnp.where(narrow, high, low)

    row_of = lax.broadcasted_iota(jnp.int32, (LOW, lanes), 0)
    count_high = pages_ref.shape[1] // chans

    def begin_row(ref, at, group, spot, i):
        number = patch[pl.ds(i, 1), :].astype(jnp.int32)
        high = lax.shift_right_logical(number, 8)
        hot = jnp.where(row_of == (number & (LOW - 1)), 1.0, 0.0).astype(jnp.bfloat16)
        values = []
        for step in range(STEPS):
            every = jnp.dot(pages_ref[step], hot, preferred_element_type=jnp.float32)
            value = every[:chans]
            for h in range(1, count_high):
                value = jnp.where(high == h, every[h * chans : (h + 1) * chans], value)
            values.append(value)
        main = ref[at].astype(jnp.float32)
        right = pltpu.roll(onright_ref[group].astype(jnp.float32), (tile_w - spot * HALO) % tile_w, 1)
        left = pltpu.roll(onleft_ref[group].astype(jnp.float32), tile_w - HALO - spot * HALO, 1)
        start = jnp.concatenate([main, jnp.where(narrow, right, left)], axis=1)
        start = start + trust[pl.ds(i, 1), :] * values[0]
        field[i + 1] = jnp.where(keep(i), start, 0.0).astype(jnp.bfloat16)
        second[i] = values[1].astype(jnp.bfloat16)

    for ref, start, size in ((above_ref, 0, HALO), (state_ref, HALO, tile_h), (below_ref, HALO + tile_h, HALO)):
        def begin_group(g, carry, ref=ref, start=start):
            for spot in range(HALO):
                at = g * HALO + spot
                begin_row(ref, at, (start + g * HALO) // per + spot // per, spot % per, start + at)
            return carry

        lax.fori_loop(0, size // HALO, begin_group, 0)

    for layer in range(STEPS * LAYERS):
        source, target = (field, inner) if layer % 2 == 0 else (inner, field)
        if layer == LAYERS:
            def again(i, carry):
                value = field[i + 1].astype(jnp.float32)
                value = value + trust[pl.ds(i, 1), :] * second[i].astype(jnp.float32)
                field[i + 1] = jnp.where(keep(i), value, 0.0).astype(jnp.bfloat16)
                return carry

            lax.fori_loop(layer, full_h - layer, again, 0)
        first = layer - layer % 2
        total = full_h - 2 * first
        unroll = max(d for d in range(1, UNROLL + 1) if total % d == 0)

        def conv_rows(g, carry, layer=layer, unroll=unroll, first=first, source=source, target=target):
            early, late = carry
            kernel = weight_ref[layer % LAYERS]
            for u in range(unroll):
                r = first + g * unroll + u
                value = source[r + 1]
                stacked = jnp.concatenate(
                    [pltpu.roll(value, 1, 1), value, pltpu.roll(value, lanes - 1, 1)], axis=0
                )
                product = jnp.dot(kernel, stacked, preferred_element_type=jnp.float32)
                done = late + product[2 * chans :]
                late = early + product[chans : 2 * chans]
                early = product[:chans]
                if layer % 2 == 0:
                    done = jnp.maximum(done, 0.0)
                else:
                    done = field[r].astype(jnp.float32) + done
                target[r] = jnp.where(keep(r - 1), done, 0.0).astype(jnp.bfloat16)
            return early, late

        zero = jnp.zeros((chans, lanes), jnp.float32)
        lax.fori_loop(0, total // unroll, conv_rows, (zero, zero))

    out_ref[...] = field[pl.ds(HALO + 1, tile_h), :, :tile_w]


def trunk(rows, cols, pages, state, above, below, onleft, onright, aux, around, weights):
    tile_h, chans, tile_w = state.shape
    full_h, lanes = tile_h + 2 * HALO, 2 * tile_w
    return pl.pallas_call(
        functools.partial(trunk_kernel, rows, cols),
        in_specs=[VMEM] * 9,
        out_specs=VMEM,
        out_shape=jax.ShapeDtypeStruct(state.shape, jnp.bfloat16),
        scratch_shapes=[
            pltpu.VMEM((full_h + 2, chans, lanes), jnp.bfloat16),
            pltpu.VMEM((full_h + 2, chans, lanes), jnp.bfloat16),
            pltpu.VMEM((full_h, chans, lanes), jnp.bfloat16),
            pltpu.VMEM((full_h, lanes), jnp.float32),
            pltpu.VMEM((full_h, lanes), jnp.float32),
        ],
        compiler_params=pltpu.CompilerParams(vmem_limit_bytes=48 * 1024 * 1024),
    )(pages, state, above, below, onleft, onright, aux, around, weights)


def packed(edge, tile_w):
    tile_h, chans, width = edge.shape
    per = tile_w // width
    return edge.reshape(tile_h // per, per, chans, width).transpose(0, 2, 1, 3).reshape(
        tile_h // per, chans, tile_w
    )


def body(rows, cols, features, patch_index, confidence, bank, page_owner, texture_weight, conv_weight):
    chans, tile_h, tile_w = features.shape
    proj = project(texture_weight, bank)
    state = features.transpose(1, 0, 2)
    left = packed(state[:, :, :HALO], tile_w)
    right = packed(state[:, :, tile_w - HALO :], tile_w)
    aux = jnp.stack([patch_index.astype(jnp.float32), confidence])
    received = exchange(rows, cols, page_owner, proj, state, left, right, aux, conv_weight)
    pages, above, below, onleft, onright, around, weights = received
    out = trunk(rows, cols, pages, state, above, below, onleft, onright, aux, around, weights)
    return out.transpose(1, 0, 2)


def solution(mesh):
    return jax.shard_map(
        functools.partial(body, mesh.shape["row"], mesh.shape["col"]),
        mesh=mesh,
        in_specs=(
            P(None, "row", "col"),
            P("row", "col"),
            P("row", "col"),
            P(("row", "col"), None, None),
            P(),
            P(),
            P(),
        ),
        out_specs=P(None, "row", "col"),
        check_vma=False,
    )
```
